256 devices in a mesh: seq: 128 (over y, z, x), head: 2 (over core).
Axes of the slice: x: 4, y: 4, z: 8, core: 2. Of those that a mesh axis runs over, the one named last changes fastest.
Arguments:
- query: bfloat16 [16384, 32, 128], P('seq', 'head'), may hold values from -6 to 6
- key: bfloat16 [16384, 4, 128], P('seq', 'head'), may hold values from -6 to 6
- value: bfloat16 [16384, 4, 128], P('seq', 'head'), may hold values from -6 to 6
- dout: bfloat16 [16384, 32, 128], P('seq', 'head'), may hold values from -0.59765625 to 0.59765625
- saved_out: bfloat16 [16384, 32, 128], P(('seq', 'head')), may hold values from -6 to 6
- saved_lse: float32 [16384, 32], P(('seq', 'head')), may hold values from 3 to 7
- row_token: int32 [16384], P(('seq', 'head')), may hold values from 0 to 16383, as said below
- token_row: int32 [16384], P('seq'), may hold values from 0 to 16383, as said below
- doc_lengths: int32 [128], replicated, may hold values from 1 to 1024, as said below
Outputs:
- dquery: bfloat16 [16384, 32, 128], P('seq', 'head')
- dkey: bfloat16 [16384, 4, 128], P('seq', 'head')
- dvalue: bfloat16 [16384, 4, 128], P('seq', 'head')
The draws below stay inside these ranges and needn't reach their ends.
Inputs may be any that keep to these rules, and one draw needn't show every extreme that they name: `doc_lengths`: documents sum to 16384 tokens; the first and longest has exactly 1024; every other has at most 256. Every token appears once; token_row is the inverse of row_token. Of the rows of one owner (one index of seq+head), at most 2 belong to the tokens of one index of seq, and some owner reaches 2. `token_row`: the inverse of row_token.
All inputs are finite; a program needn't handle non-finite values.
Results may differ from the reference program's by a relative error of at most 0.0055.
Values may be sent and summed in bfloat16 or wider, within the bound.
A program may use at most 64 MiB of HBM per device.

```python
import jax
import jax.numpy as jnp
from jax import lax

QUERY_HEADS = 32
KEY_VALUE_HEADS = 4
HEAD_SIZE = 128
SHARD_TOKENS = 128
SPAN = 8
PACKED_TOKENS = 16384
MOST = 1024
CAP = 2
N_SEQ = 128
N_HEAD = 2


def routing_plan(key):
    own_rows = SHARD_TOKENS // N_HEAD
    pairs = own_rows // CAP
    query_groups = 2 * pairs
    first = jax.random.randint(jax.random.fold_in(key, 11), (N_HEAD, pairs), 0, CAP + 1)
    first = first.at[:, 0].set(CAP)
    sizes = jnp.stack([first, CAP - first], axis=-1).reshape(N_HEAD, query_groups).astype(jnp.int32)
    starts = (jnp.cumsum(sizes, axis=1) - sizes).astype(jnp.int32)
    head_keys = jax.random.split(jax.random.fold_in(key, 12), N_HEAD)
    others = jax.vmap(lambda k: jax.random.permutation(k, N_SEQ - 3)[:query_groups - 1])(head_keys).astype(jnp.int32)
    others = others + 2
    others = jnp.where(others >= N_SEQ // 2, others + 1, others)
    head_ids = jnp.arange(N_HEAD, dtype=jnp.int32)
    lead = jnp.where(head_ids % 2 == 0, 1, N_SEQ // 2).astype(jnp.int32)
    offsets = jnp.concatenate([lead[:, None], others], axis=1).astype(jnp.int32)
    slot = jnp.arange(own_rows, dtype=jnp.int32)
    group_of = jnp.sum((starts[:, None, :] <= slot[None, :, None]).astype(jnp.int32), axis=2) - 1
    shift_of = jnp.take_along_axis(offsets, group_of, axis=1)
    seq_ids = jnp.arange(N_SEQ, dtype=jnp.int32)
    dest = (seq_ids[:, None, None] + shift_of[None, :, :]) % N_SEQ
    token_keys = jax.random.split(jax.random.fold_in(key, 13), N_SEQ)
    token_perm = jax.vmap(lambda k: jax.random.permutation(k, SHARD_TOKENS))(token_keys).astype(jnp.int32)
    incoming = head_ids[None, :, None] * own_rows + slot[None, None, :]
    incoming = jnp.broadcast_to(incoming, dest.shape)
    token = dest * SHARD_TOKENS + token_perm[dest, incoming]
    row_keys = jax.random.split(jax.random.fold_in(key, 14), N_SEQ * N_HEAD)
    row_perm = jax.vmap(lambda k: jax.random.permutation(k, own_rows))(row_keys).astype(jnp.int32)
    owner = seq_ids[:, None] * N_HEAD + head_ids[None, :]
    row = owner[:, :, None] * own_rows + row_perm.reshape(N_SEQ, N_HEAD, own_rows)
    row_token = jnp.zeros((PACKED_TOKENS,), jnp.int32).at[row.ravel()].set(token.ravel())
    token_row = jnp.zeros((PACKED_TOKENS,), jnp.int32).at[token.ravel()].set(row.ravel())
    return (row_token, token_row)


def draw_row_token(key, part):
    return routing_plan(key)[0]


def draw_token_row(key, part):
    return routing_plan(key)[1]


def draw_doc_lengths(key, part):
    key = jax.random.fold_in(key, 21)
    remain = (N_SEQ - SPAN) * SHARD_TOKENS
    pieces = N_SEQ - 1
    stride = max(1, remain // pieces)
    inner = jnp.arange(1, pieces, dtype=jnp.int32)
    base = inner * remain // pieces
    jitter = jax.random.randint(key, (pieces - 1,), 0, stride).astype(jnp.int32)
    cuts = jnp.concatenate([jnp.zeros((1,), jnp.int32), base + jitter, jnp.full((1,), remain, jnp.int32)])
    rest = (cuts[1:] - cuts[:-1]).astype(jnp.int32)
    return jnp.concatenate([jnp.full((1,), MOST, jnp.int32), rest]).astype(jnp.int32)


def block_levels(own_key, extent, cuts, least, largest):
    loudness, own = 1.0, jax.random.fold_in(own_key, 6)
    for dim, shards_of in cuts:
        heights = jnp.exp(jax.random.uniform(jax.random.fold_in(own, dim), (shards_of,), jnp.float32, least / len(cuts), largest / len(cuts)))
        loudness = loudness * jnp.repeat(heights, extent[dim] // shards_of).reshape([-1 if axis == dim else 1 for axis in range(len(extent))])
    return loudness


def bell_draw(key, extent, spread, most, cuts=(), kind=jnp.bfloat16):
    drawn = spread * jax.random.normal(key, extent, jnp.float32)
    if cuts:
        drawn = drawn * block_levels(key, extent, cuts, -0.22, 0.18)
    return jnp.clip(drawn, -most, most).astype(kind)


def setup_inputs(seed: int = 0) -> dict:
    keys = jax.random.split(jax.random.key(seed), 10)
    query = bell_draw(keys[0], (PACKED_TOKENS, QUERY_HEADS, HEAD_SIZE), 1.0, 6.0, ((0, 128), (1, 2)))
    key = bell_draw(keys[1], (PACKED_TOKENS, KEY_VALUE_HEADS, HEAD_SIZE), 1.0, 6.0, ((0, 128), (1, 2)))
    value = bell_draw(keys[2], (PACKED_TOKENS, KEY_VALUE_HEADS, HEAD_SIZE), 1.0, 6.0, ((0, 128), (1, 2)))
    dout = bell_draw(keys[3], (PACKED_TOKENS, QUERY_HEADS, HEAD_SIZE), 0.1, 0.59765625, ((0, 128), (1, 2)))
    saved_out = bell_draw(keys[4], (PACKED_TOKENS, QUERY_HEADS, HEAD_SIZE), 1.0, 6.0, ((0, 256),))
    saved_lse = jnp.clip(3.0 + 4.0 * jax.random.uniform(keys[5], (PACKED_TOKENS, QUERY_HEADS), jnp.float32) ** block_levels(keys[5], (PACKED_TOKENS, QUERY_HEADS), ((0, 256),), -0.2, 0.2), 3.0, 7.0)
    row_token = draw_row_token(jax.random.fold_in(keys[9], 71), 0)
    token_row = draw_token_row(jax.random.fold_in(keys[9], 71), 0)
    doc_lengths = draw_doc_lengths(jax.random.fold_in(keys[9], 71), 0)
    return dict(query=query, key=key, value=value, dout=dout, saved_out=saved_out, saved_lse=saved_lse, row_token=row_token, token_row=token_row, doc_lengths=doc_lengths)


def doc_index(positions, doc_lengths):
    ends = jnp.cumsum(doc_lengths).astype(jnp.int32)
    return jnp.sum((ends[None, :] <= positions[:, None]).astype(jnp.int32), axis=1).astype(jnp.int32)


def block_grads(qgroup, dgroup, lse_t, delta_t, qpos, qdoc, kblock, vblock, kpos, kdoc, scale):
    f32 = jnp.float32
    scores = jnp.einsum('ihgd,jhd->hgij', qgroup.astype(f32), kblock.astype(f32)) * scale
    allowed = (kdoc[None, :] == qdoc[:, None]) & (kpos[None, :] <= qpos[:, None])
    probs = jnp.where(allowed[None, None], jnp.exp(scores - lse_t), 0.0)
    probs_b = lax.optimization_barrier(probs.astype(jnp.bfloat16))
    dval = jnp.einsum('hgij,ihgd->jhd', probs_b.astype(f32), dgroup.astype(f32))
    dprobs = jnp.einsum('ihgd,jhd->hgij', dgroup.astype(f32), vblock.astype(f32))
    dscores = lax.optimization_barrier((probs * (dprobs - delta_t)).astype(jnp.bfloat16))
    dq = jnp.einsum('hgij,jhd->ihgd', dscores.astype(f32), kblock.astype(f32)) * scale
    dk = jnp.einsum('hgij,ihgd->jhd', dscores.astype(f32), qgroup.astype(f32)) * scale
    return dq, dk, dval


def reference(query, key, value, dout, saved_out, saved_lse, row_token, token_row, doc_lengths):
    query_groups = QUERY_HEADS // KEY_VALUE_HEADS
    scale = HEAD_SIZE ** -0.5
    out_tok = jnp.zeros_like(saved_out).at[row_token].set(saved_out)
    token_logsumexp = saved_lse[token_row]
    output_dot_gradient = jnp.sum(dout.astype(jnp.float32) * out_tok.astype(jnp.float32), axis=-1)
    docs = doc_index(jnp.arange(PACKED_TOKENS, dtype=jnp.int32), doc_lengths)
    padding_amount = SPAN * SHARD_TOKENS
    window_width = (SPAN + 1) * SHARD_TOKENS
    padded_keys = jnp.concatenate([jnp.zeros((padding_amount, KEY_VALUE_HEADS, HEAD_SIZE), key.dtype), key], axis=0)
    padded_values = jnp.concatenate([jnp.zeros((padding_amount, KEY_VALUE_HEADS, HEAD_SIZE), value.dtype), value], axis=0)
    dpad = jnp.concatenate([jnp.full((padding_amount,), -1, jnp.int32), docs], axis=0)

    def visit(carry, blk):
        dkp, dvp = carry
        start_offset = (blk * SHARD_TOKENS).astype(jnp.int32)
        query_block = lax.dynamic_slice_in_dim(query, start_offset, SHARD_TOKENS, 0).reshape(SHARD_TOKENS, KEY_VALUE_HEADS, query_groups, HEAD_SIZE)
        document_bounds = lax.dynamic_slice_in_dim(dout, start_offset, SHARD_TOKENS, 0).reshape(SHARD_TOKENS, KEY_VALUE_HEADS, query_groups, HEAD_SIZE)
        lower_bounds = lax.dynamic_slice_in_dim(token_logsumexp, start_offset, SHARD_TOKENS, 0).reshape(SHARD_TOKENS, KEY_VALUE_HEADS, query_groups).transpose(1, 2, 0)[..., None]
        end_bounds = lax.dynamic_slice_in_dim(output_dot_gradient, start_offset, SHARD_TOKENS, 0).reshape(SHARD_TOKENS, KEY_VALUE_HEADS, query_groups).transpose(1, 2, 0)[..., None]
        qpos = start_offset + jnp.arange(SHARD_TOKENS, dtype=jnp.int32)
        qdoc = lax.dynamic_slice_in_dim(docs, start_offset, SHARD_TOKENS, 0)
        kb = lax.dynamic_slice_in_dim(padded_keys, start_offset, window_width, 0)
        value_block = lax.dynamic_slice_in_dim(padded_values, start_offset, window_width, 0)
        kdoc = lax.dynamic_slice_in_dim(dpad, start_offset, window_width, 0)
        kpos = start_offset - padding_amount + jnp.arange(window_width, dtype=jnp.int32)
        dq, dk, dv = block_grads(query_block, document_bounds, lower_bounds, end_bounds, qpos, qdoc, kb, value_block, kpos, kdoc, scale)
        dkp = lax.dynamic_update_slice_in_dim(dkp, lax.dynamic_slice_in_dim(dkp, start_offset, window_width, 0) + dk, start_offset, 0)
        dvp = lax.dynamic_update_slice_in_dim(dvp, lax.dynamic_slice_in_dim(dvp, start_offset, window_width, 0) + dv, start_offset, 0)
        return (dkp, dvp), dq

    zero_fill = jnp.zeros((padding_amount + PACKED_TOKENS, KEY_VALUE_HEADS, HEAD_SIZE), jnp.float32)
    (dkp, dvp), dqs = lax.scan(visit, (zero_fill, zero_fill), jnp.arange(PACKED_TOKENS // SHARD_TOKENS, dtype=jnp.int32))
    dquery = dqs.reshape(PACKED_TOKENS, QUERY_HEADS, HEAD_SIZE).astype(jnp.bfloat16)
    return dquery, dkp[padding_amount:].astype(jnp.bfloat16), dvp[padding_amount:].astype(jnp.bfloat16)
```

```python
import functools

import jax
import jax.numpy as jnp
from jax import lax
from jax.experimental import pallas as pl
from jax.experimental.pallas import tpu as pltpu
from jax.sharding import PartitionSpec as P

MESH = pl.DeviceIdType.MESH
f32 = jnp.float32
bf16 = jnp.bfloat16
i32 = jnp.int32

TOK = 128
ROWS = 64
CAP = 2
FIRST = 8
REACH = 2
HEADS = 16
GROUPS = 2
QG = 8
D = 128
SCALE = D ** (-0.5)


def kernel(
    n, meta_ref, lse_ref, q_ref, do_ref, k_ref, v_ref, out_ref,
    dq_ref, dk_ref, dv_ref,
    idx_v, idx_s, send, recv, lsend, lrecv, lmat, lse_t, start_row,
    wide, qh, qt, doh, dot_, kr, vr, pbuf, dpbuf, pb, dvs, dvr, dks, dkr, dk0, dqt, delta_t,
    s_idx, s_out, r_out, s_lse, r_lse, s_kv, r_kv, s_dv, r_dv, s_dk, r_dk,
):
    s = lax.axis_index("seq")
    h = lax.axis_index("head")
    me = s * 2 + h
    peers = 2 * n - 1

    barrier = pltpu.get_barrier_semaphore()

    def hello(i, c):
        d = lax.rem(s + i, n)
        for o in range(2):
            pl.semaphore_signal(barrier, inc=1, device_id=(d, o), device_id_type=MESH)
        return c

    lax.fori_loop(1, n, hello, 0)
    pl.semaphore_signal(barrier, inc=1, device_id=(s, 1 - h), device_id_type=MESH)

    sub = lax.broadcasted_iota(i32, (TOK, 128), 0)
    lane = lax.broadcasted_iota(i32, (TOK, 128), 1)
    one = jnp.ones((TOK, 128), i32)
    none = jnp.zeros((TOK, 128), i32)
    tgt_r = jnp.broadcast_to(meta_ref[0:1, :] >> 7, (TOK, 128))
    tgt_c = jnp.transpose(tgt_r)
    same = (tgt_r == tgt_c) & (lane < sub)
    rank_c = jnp.sum(jnp.where(same, one, none), axis=1, keepdims=True)
    slot_c = jnp.where(sub < ROWS, tgt_c * CAP + rank_c, -one)
    for half in range(2):
        hit = slot_c == lane + 128 * half
        row = jnp.sum(jnp.where(hit, sub, none), axis=0, keepdims=True)
        idx_v[half : half + 1, :] = jnp.clip(row, 0, ROWS - 1)
    tr_r = jnp.broadcast_to(meta_ref[1:2, :], (TOK, 128))
    own_r = tr_r >> 6
    tr_c = jnp.transpose(tr_r)
    own_c = jnp.transpose(own_r)
    both = own_r == own_c
    trank_r = jnp.sum(jnp.where(both & (tr_c < tr_r), one, none), axis=0, keepdims=True)
    trank_c = jnp.sum(jnp.where(both & (tr_r < tr_c), one, none), axis=1, keepdims=True)
    idx_v[2:3, :] = jnp.clip(own_r[0:1, :], 0, 2 * n - 1)
    idx_v[3:4, :] = jnp.clip(own_r[0:1, :] * CAP + trank_r, 0, 4 * n - 1)
    idx_v[4:8, :] = jnp.zeros((4, 128), i32)
    to_smem = pltpu.make_async_copy(idx_v, idx_s, s_idx)
    to_smem.start()

    len_r = jnp.broadcast_to(meta_ref[2:3, :], (TOK, 128)).astype(f32)
    ends_c = jnp.sum(jnp.where(lane <= sub, len_r, 0.0), axis=1, keepdims=True)
    pos_r = (lane + s * TOK).astype(f32)
    start_row[...] = jnp.max(jnp.where(ends_c <= pos_r, ends_c, 0.0), axis=0, keepdims=True)

    kr[0] = k_ref[...]
    vr[0] = v_ref[...]
    to_smem.wait()
    pl.semaphore_wait(barrier, peers)

    def feeds(a, jj):
        return (a + jj < n) & ((a + jj < FIRST) | ((a >= FIRST) & (jj <= REACH)))

    def kv_copy(which, jj):
        return pltpu.make_async_remote_copy(
            src_ref=(k_ref, v_ref)[which], dst_ref=(kr, vr)[which].at[jj],
            send_sem=s_kv.at[which, jj], recv_sem=r_kv.at[which, jj],
            device_id=(lax.rem(s + jj, n), h), device_id_type=MESH,
        )

    for jj in range(1, FIRST):
        @pl.when(feeds(s, jj))
        def _():
            kv_copy(0, jj).start()
            kv_copy(1, jj).start()

    def slot_row(k):
        return jnp.clip(idx_s[k // 128, lax.rem(k, 128)], 0, ROWS - 1)

    lane1 = lax.broadcasted_iota(i32, (1, 128), 1)

    def lse_row(d):
        return jnp.where(lane1 < 32, lse_ref[pl.ds(slot_row(2 * d), 1), :], lse_ref[pl.ds(slot_row(2 * d + 1), 1), :])

    def lse_copy(d, o):
        return pltpu.make_async_remote_copy(
            src_ref=lsend.at[d], dst_ref=lrecv.at[me], send_sem=s_lse, recv_sem=r_lse,
            device_id=(d, o), device_id_type=MESH,
        )

    def send_lse(i, c):
        d = lax.rem(s + i, n)
        lsend[d] = lse_row(d)
        lse_copy(d, 0).start()
        lse_copy(d, 1).start()
        return c

    lax.fori_loop(1, n, send_lse, 0)
    own_lse = lse_row(s)
    lsend[s] = own_lse
    lrecv[me] = own_lse
    lse_copy(s, 1 - h).start()

    def out_copy(d, o):
        return pltpu.make_async_remote_copy(
            src_ref=send.at[pl.ds(4 * d + 2 * o, 2)], dst_ref=recv.at[pl.ds(2 * me, 2)],
            send_sem=s_out, recv_sem=r_out, device_id=(d, o), device_id_type=MESH,
        )

    def fill(d):
        for k in range(CAP):
            r = slot_row(2 * d + k)
            for o in range(2):
                send[4 * d + 2 * o + k] = out_ref[r, o * HEADS : (o + 1) * HEADS, :]

    def send_out(i, c):
        d = lax.rem(s + i, n)
        fill(d)
        out_copy(d, 0).start()
        out_copy(d, 1).start()
        return c

    lax.fori_loop(1, n, send_out, 0)
    fill(s)
    out_copy(s, 1 - h).start()
    for k in range(CAP):
        recv[2 * me + k] = send[4 * s + 2 * h + k]

    for src, nat, tra in ((q_ref, qh, qt), (do_ref, doh, dot_)):
        wide[0 : TOK * HEADS] = src[...].astype(f32).reshape(TOK * HEADS, D)
        for hh in range(HEADS):
            x = wide[pl.ds(hh, TOK, stride=HEADS), :]
            g, m = hh // QG, hh % QG
            nat[g, m * TOK : (m + 1) * TOK, :] = x.astype(bf16)
            tra[g, :, m * TOK : (m + 1) * TOK] = jnp.transpose(x).astype(bf16)

    def lse_total():
        return pltpu.make_async_remote_copy(
            src_ref=lsend_all.at[pl.ds(0, peers)], dst_ref=lrecv.at[pl.ds(0, peers)], send_sem=s_lse, recv_sem=r_lse,
            device_id=(s, 1 - h), device_id_type=MESH,
        )

    lsend_all = lrecv
    lse_total().wait_recv()

    def pick_lse(t, c):
        lmat[pl.ds(t, 1), :] = lrecv[jnp.clip(idx_s[2, t], 0, 2 * n - 1)]
        return c

    lax.fori_loop(0, TOK, pick_lse, 0)
    m = lmat[...]
    m = jnp.where(trank_c == 0, m, pltpu.roll(m, 128 - 32, 1))
    m = jnp.where(h == 0, m, pltpu.roll(m, 128 - 16, 1))
    lse_t[...] = jnp.transpose(m)

    blocks = jnp.where(s < FIRST, s + 1, jnp.minimum(s - FIRST, REACH) + 1)

    def back(bufs, bufr, ss, rs, jj):
        return pltpu.make_async_remote_copy(
            src_ref=bufs.at[jj], dst_ref=bufr.at[jj], send_sem=ss.at[jj], recv_sem=rs.at[jj],
            device_id=(lax.rem(s - jj + n, n), h), device_id_type=MESH,
        )

    def ahead(jj, c):
        @pl.when(jj > 0)
        def _():
            kv_copy(0, jj).wait_recv()
            kv_copy(1, jj).wait_recv()

        key_pos = (sub + (s - jj) * TOK).astype(f32)
        allowed = (key_pos <= pos_r) & (key_pos >= start_row[...])
        for g in range(GROUPS):
            k = kr[jj, :, g * D : (g + 1) * D]
            v = vr[jj, :, g * D : (g + 1) * D]
            st = jnp.dot(k, qt[g], preferred_element_type=f32)
            for m in range(QG):
                hh = g * QG + m
                cols = slice(m * TOK, (m + 1) * TOK)
                p = jnp.where(allowed, jnp.exp(st[:, cols] * SCALE - lse_t[hh : hh + 1, :]), 0.0)
                pbuf[jj, g, :, cols] = p
                pb[:, cols] = p.astype(bf16)
            dpbuf[jj, g] = jnp.dot(v, dot_[g], preferred_element_type=f32)
            dvs[jj, :, g * D : (g + 1) * D] = jnp.dot(pb[...], doh[g], preferred_element_type=f32)

        @pl.when(jj > 0)
        def _():
            back(dvs, dvr, s_dv, r_dv, jj).start()

        return c

    lax.fori_loop(0, blocks, ahead, 0)

    dv = dvs[0]
    dk0[...] = dv
    for jj in range(1, FIRST):
        @pl.when(feeds(s, jj))
        def _():
            back(dvs, dvr, s_dv, r_dv, jj).wait_recv()
            dk0[...] += dvr[jj]
    dv_ref[...] = dk0[...].astype(bf16)

    dqt[...] = jnp.zeros_like(dqt)

    out_total = pltpu.make_async_remote_copy(
        src_ref=recv.at[pl.ds(0, 2 * peers)], dst_ref=recv.at[pl.ds(0, 2 * peers)], send_sem=s_out, recv_sem=r_out,
        device_id=(s, 1 - h), device_id_type=MESH,
    )
    out_total.wait_recv()

    def products(t, c):
        x = recv[jnp.clip(idx_s[3, t], 0, 4 * n - 1)].astype(f32) * do_ref[t].astype(f32)
        wide[pl.ds(pl.multiple_of(t * HEADS, HEADS), HEADS), :] = x
        return c

    lax.fori_loop(0, TOK, products, 0)
    acc = jnp.zeros((TOK, 128), f32)
    for hh in range(HEADS):
        x = jnp.sum(wide[pl.ds(hh, TOK, stride=HEADS), :], axis=1, keepdims=True)
        acc = jnp.where(lane == hh, x, acc)
    delta_t[...] = jnp.transpose(acc)

    def after(i, c):
        jj = blocks - 1 - i
        for g in range(GROUPS):
            k = kr[jj, :, g * D : (g + 1) * D]
            for m in range(QG):
                hh = g * QG + m
                cols = slice(m * TOK, (m + 1) * TOK)
                pb[:, cols] = (pbuf[jj, g, :, cols] * (dpbuf[jj, g, :, cols] - delta_t[hh : hh + 1, :])).astype(bf16)
            ds = pb[...]
            dk0[:, g * D : (g + 1) * D] = jnp.dot(ds, qh[g], preferred_element_type=f32) * SCALE
            kt = jnp.transpose(k.astype(f32)).astype(bf16)
            dqt[g] += jnp.dot(kt, ds, preferred_element_type=f32)

        @pl.when(jj > 0)
        def _():
            dks[jj] = dk0[...].astype(bf16)
            back(dks, dkr, s_dk, r_dk, jj).start()

        return c

    lax.fori_loop(0, blocks, after, 0)

    for hh in range(HEADS):
        g, m = hh // QG, hh % QG
        wide[pl.ds(hh, TOK, stride=HEADS), :] = jnp.transpose(dqt[g, :, m * TOK : (m + 1) * TOK]) * SCALE
    dq_ref[...] = wide[0 : TOK * HEADS].reshape(TOK, HEADS, D).astype(bf16)

    for jj in range(1, FIRST):
        @pl.when(feeds(s, jj))
        def _():
            back(dks, dkr, s_dk, r_dk, jj).wait_recv()
            dk0[...] += dkr[jj].astype(f32)
    dk_ref[...] = dk0[...].astype(bf16)

    lse_total().wait_send()
    out_total.wait_send()
    for jj in range(1, FIRST):
        @pl.when(feeds(s, jj))
        def _():
            kv_copy(0, jj).wait_send()
            kv_copy(1, jj).wait_send()

        @pl.when(jj < blocks)
        def _():
            back(dvs, dvr, s_dv, r_dv, jj).wait_send()
            back(dks, dkr, s_dk, r_dk, jj).wait_send()


def shards(query, key, value, dout, saved_out, saved_lse, row_token, token_row, doc_lengths):
    n = lax.axis_size("seq")
    meta = jnp.stack([jnp.pad(row_token, (0, TOK - ROWS), constant_values=-1), token_row, doc_lengths])
    lse4 = jnp.concatenate([saved_lse] * 4, axis=1)
    k2 = key.reshape(TOK, GROUPS * D)
    v2 = value.reshape(TOK, GROUPS * D)
    vm = pl.BlockSpec(memory_space=pltpu.VMEM)
    dma = pltpu.SemaphoreType.DMA
    dq, dk, dv = pl.pallas_call(
        functools.partial(kernel, n),
        out_shape=(
            jax.ShapeDtypeStruct((TOK, HEADS, D), bf16),
            jax.ShapeDtypeStruct((TOK, GROUPS * D), bf16),
            jax.ShapeDtypeStruct((TOK, GROUPS * D), bf16),
        ),
        in_specs=[vm] * 7,
        out_specs=(vm, vm, vm),
        scratch_shapes=[
            pltpu.VMEM((8, 128), i32),
            pltpu.SMEM((8, 128), i32),
            pltpu.VMEM((4 * n, HEADS, D), bf16),
            pltpu.VMEM((4 * n, HEADS, D), bf16),
            pltpu.VMEM((n, 1, 128), f32),
            pltpu.VMEM((2 * n, 1, 128), f32),
            pltpu.VMEM((TOK, 128), f32),
            pltpu.VMEM((128, TOK), f32),
            pltpu.VMEM((1, 128), f32),
            pltpu.VMEM((TOK * HEADS + HEADS, D), f32),
            pltpu.VMEM((GROUPS, QG * TOK, D), bf16),
            pltpu.VMEM((GROUPS, D, QG * TOK), bf16),
            pltpu.VMEM((GROUPS, QG * TOK, D), bf16),
            pltpu.VMEM((GROUPS, D, QG * TOK), bf16),
            pltpu.VMEM((FIRST, TOK, GROUPS * D), bf16),
            pltpu.VMEM((FIRST, TOK, GROUPS * D), bf16),
            pltpu.VMEM((FIRST, GROUPS, TOK, QG * TOK), f32),
            pltpu.VMEM((FIRST, GROUPS, TOK, QG * TOK), f32),
            pltpu.VMEM((TOK, QG * TOK), bf16),
            pltpu.VMEM((FIRST, TOK, GROUPS * D), f32),
            pltpu.VMEM((FIRST, TOK, GROUPS * D), f32),
            pltpu.VMEM((FIRST, TOK, GROUPS * D), bf16),
            pltpu.VMEM((FIRST, TOK, GROUPS * D), bf16),
            pltpu.VMEM((TOK, GROUPS * D), f32),
            pltpu.VMEM((GROUPS, D, QG * TOK), f32),
            pltpu.VMEM((128, TOK), f32),
            dma, dma, dma, dma, dma,
            dma((2, FIRST)), dma((2, FIRST)),
            dma((FIRST,)), dma((FIRST,)), dma((FIRST,)), dma((FIRST,)),
        ],
        compiler_params=pltpu.CompilerParams(
            collective_id=0, has_side_effects=True, vmem_limit_bytes=58 * 1024 * 1024
        ),
        name="grads",
    )(meta, lse4, query, dout, k2, v2, saved_out)
    return dq, dk.reshape(TOK, GROUPS, D), dv.reshape(TOK, GROUPS, D)


def solution(mesh):
    placed = (
        P("seq", "head", None),
        P("seq", "head", None),
        P("seq", "head", None),
        P("seq", "head", None),
        P(("seq", "head"), None, None),
        P(("seq", "head"), None),
        P(("seq", "head")),
        P("seq"),
        P(),
    )
    return jax.shard_map(
        shards,
        mesh=mesh,
        in_specs=placed,
        out_specs=(P("seq", "head", None), P("seq", "head", None), P("seq", "head", None)),
        check_vma=False,
    )
```
